128 devices in a mesh: slab: 4 (over y), cube: 32 (over x, z, core).
Axes of the slice: x: 4, y: 4, z: 4, core: 2. Of those that a mesh axis runs over, the one named last changes fastest.
Arguments:
- owned_part: bfloat16 [4096, 64, 384], P(('slab', 'cube')), may hold values from -6 to 6
- shared_part: bfloat16 [4096, 64, 384], P(('slab', 'cube')), may hold values from -6 to 6
- shared_cube: int32 [4096, 1], P(('slab', 'cube')), may hold values from 0 to 31; in each aligned block of 32 rows (0 to 31, 32 to 63, ...) at most 2 rows name the same one
- shared_octant: int32 [4096], P(('slab', 'cube')), may hold values from 0 to 31
- interaction: int32 [4096, 4, 8], P(('slab', 'cube')), may hold values from 0 to 31
- operators: bfloat16 [32, 384, 384], replicated, may hold values from -0.0546875 to 0.0546875
Outputs:
- far_field: bfloat16 [4096, 64, 384], P(('slab', 'cube'))
The draws below stay inside these ranges and needn't reach their ends.
Inputs may be any that keep to these rules, and one draw needn't show every extreme that they name: `shared_cube`: among the 32 rows of one device no cube index is named by more than 2 rows, and some cube index is named by exactly 2 rows.
All inputs are finite; a program needn't handle non-finite values.
Results may differ from the reference program's by a relative error of at most 0.0048.
Values may be sent and summed in bfloat16 or wider, within the bound.
A program may use at most 256 MiB of HBM per device.

```python
import math
import jax
import jax.numpy as jnp
import numpy as np

P_SIZE = 384
R = 64
OCT = 32
LPS = 8
CAP = 2
SLOTS = 32
NOPS = 32
OCTANTS = 4096
N_SLAB = 4
N_CUBE = 32
DEVICES = 128


def plant(array, own_key, least, largest):
    index_at = [jax.random.randint(jax.random.fold_in(own_key, axis), (), 0, length) for axis, length in enumerate(array.shape)]
    main_axis = array.shape.index(max(array.shape))
    next_to = index_at[:main_axis] + [(index_at[main_axis] + 1) % array.shape[main_axis]] + index_at[main_axis + 1:]
    return array.at[tuple(index_at)].set(least).at[tuple(next_to)].set(largest)


def block_scale(key, shape, cuts, least, largest):
    level, own = 1.0, jax.random.fold_in(key, 6)
    for position, blocks in cuts:
        draws = jnp.exp(jax.random.uniform(jax.random.fold_in(own, position), (blocks,), jnp.float32, least / len(cuts), largest / len(cuts)))
        level = level * jnp.repeat(draws, shape[position] // blocks).reshape([-1 if axis == position else 1 for axis in range(len(shape))])
    return level


def routed_block(rng, own, number, rows, number_of, top, bound, slope):
    sequence = jax.random.permutation(rng, number_of)
    packed, common = portions_of(number_of, rows * top, bound, slope, True), portions_of(number_of, rows * top, bound, slope, False)
    places = jnp.arange(number_of)

    def named(sizes, turn):
        used = int((sizes > 0).sum())
        fixed = max(1, used // 4)
        shifted = fixed + (places - fixed + turn * (used - fixed)) % max(1, number_of - fixed)
        return jnp.zeros((number_of,), jnp.int32).at[sequence[jnp.where(places < fixed, places, shifted)]].set(jnp.asarray(sizes, jnp.int32))

    sizes = jnp.where(number % 4 == 0, named(packed, number // 4), named(common, number - number // 4 - 1))
    mixed = jax.random.permutation(jax.random.fold_in(own, 3), number_of)
    source_of, sink = mixed[0:number_of // 2 * 2:2], mixed[1:number_of // 2 * 2:2]
    slack = jnp.minimum(sizes[source_of] - 1, bound - sizes[sink]) // 2
    slack = jnp.where((source_of == sequence[0]) | (sink == sequence[0]) | (sizes[sink] == 0), 0, jnp.maximum(slack, 0))
    shifted = jax.random.randint(jax.random.fold_in(own, 4), (number_of // 2,), 0, 1 << 20) % (slack + 1)
    sizes = sizes.at[source_of].add(-shifted).at[sink].add(shifted)
    members = jnp.searchsorted(jnp.cumsum(sizes), jnp.arange(rows * top), side="right").astype(jnp.int32)
    table = members.reshape(top, rows).T
    table = table[jax.random.permutation(jax.random.fold_in(own, 1), rows)]
    turn = jax.random.randint(jax.random.fold_in(own, 2), (rows, 1), 0, top)
    return jnp.take_along_axis(table, (jnp.arange(top)[None, :] + turn) % top, axis=1)


def portions_of(count, total, most, slope, full):
    loads = [(1 << 20) // math.isqrt(standing ** slope) + 1 for standing in range(1, count + 1)]
    largest = most if full else min(most, max(-(-total // count), total * loads[0] // sum(loads)))
    least = 1 if total - largest >= count - 1 else 0
    given, surplus = [largest] + [least] * (count - 1), total - largest - least * (count - 1)
    while surplus > 0:
        candidates = [i for i in range(1, count) if given[i] < largest] or [i for i in range(1, count) if given[i] < most]
        pool, budget = sum([loads[i] for i in candidates]), surplus
        for i in candidates:
            addition = min(most - given[i], max(1, budget * loads[i] // pool), surplus)
            given[i] = given[i] + addition
            surplus = surplus - addition
    return np.array(given)


def gaussian(key, dims, scale, most, split=(), kind=jnp.bfloat16):
    values = scale * jax.random.normal(key, dims, jnp.float32)
    if split:
        values = values * block_scale(key, dims, split, -0.22, 0.18)
    return jnp.clip(values, -most, most).astype(kind)


def setup_inputs(seed: int = 0) -> dict:
    keys = jax.random.split(jax.random.key(seed), 7)
    owned_part = gaussian(keys[0], (OCTANTS, R, P_SIZE), 1.0, 6.0, ((0, 128),))
    shared_part = gaussian(keys[1], (DEVICES * SLOTS, R, P_SIZE), 1.0, 6.0, ((0, 128),))
    shared_cube_keys = jax.random.split(jax.random.fold_in(keys[2], 1), (DEVICES * SLOTS) // SLOTS)
    shared_cube_turns = jax.random.permutation(jax.random.fold_in(keys[2], 3), (DEVICES * SLOTS) // SLOTS)
    shared_cube = jax.vmap(lambda own, number: routed_block(jax.random.fold_in(keys[2], 2), own, number, SLOTS, N_CUBE, 1, CAP, 2))(shared_cube_keys, shared_cube_turns).reshape((DEVICES * SLOTS, 1))
    shared_octant = plant(jax.random.randint(keys[3], (DEVICES * SLOTS,), 0, OCT), jax.random.fold_in(keys[3], 1), 0, OCT - 1).astype(jnp.int32)
    interaction = plant(jax.random.randint(keys[4], (OCTANTS, N_SLAB, LPS), 0, OCT), jax.random.fold_in(keys[4], 1), 0, OCT - 1).astype(jnp.int32)
    operators = gaussian(keys[5], (NOPS, P_SIZE, P_SIZE), (P_SIZE * NOPS) ** -0.5, 0.0546875)
    return dict(owned_part=owned_part, shared_part=shared_part, shared_cube=shared_cube, shared_octant=shared_octant, interaction=interaction, operators=operators)


def reference(owned_part, shared_part, shared_cube, shared_octant, interaction, operators):
    slot_ids = jnp.arange(DEVICES * SLOTS, dtype=jnp.int32)
    slot_device = slot_ids // SLOTS
    slot_slab = slot_device // N_CUBE
    targets = (slot_slab * N_CUBE + shared_cube[:, 0]) * OCT + shared_octant
    summed = owned_part.astype(jnp.float32) + jax.ops.segment_sum(
        shared_part.astype(jnp.float32), targets, num_segments=OCTANTS)
    density = summed.astype(jnp.bfloat16)
    octant_ids = jnp.arange(OCTANTS, dtype=jnp.int32)
    octant_cube = (octant_ids // OCT) % N_CUBE
    far_field = jnp.zeros((OCTANTS * R, P_SIZE), jnp.float32)
    for source_slab in range(N_SLAB):
        for entry in range(LPS):
            sources = (source_slab * N_CUBE + octant_cube) * OCT + interaction[:, source_slab, entry]
            selected = density[sources].reshape(OCTANTS * R, P_SIZE)
            far_field = far_field + jnp.dot(selected, operators[source_slab * LPS + entry],
                                            preferred_element_type=jnp.float32)
    return far_field.reshape(OCTANTS, R, P_SIZE).astype(jnp.bfloat16)
```

```python
import functools

import jax
import jax.numpy as jnp
from jax import lax
from jax.experimental import pallas as pl
from jax.experimental.pallas import tpu as pltpu
from jax.sharding import PartitionSpec as P

CAP = 2
ROWS = 16
MESH = pl.DeviceIdType.MESH


def kernel(
    tab, inter_s, inter_v, keys, shared, owned, ops, out,
    sh0, sh1, sh2, sh3, ow, opv, send, recv, keyr, kron, dn, dp, y, pbs, pbr, acc, outb, ipv, ips,
    sh_sem, ow_sem, op_sem, send_sem, recv_sem, ksend_sem, krecv_sem,
    isend_sem, irecv_sem, ips_sem, as_sem, ar_sem, bs_sem, br_sem, out_sem,
):
    sh = (sh0, sh1, sh2, sh3)
    chunks, octs, rows, width = dn.shape
    peers = recv.shape[1]
    lps = opv.shape[1]
    slab = lax.axis_index("slab")
    cube = lax.axis_index("cube")
    x, z, core = cube // 8, (cube // 2) % 4, cube % 2
    swap = slab + 1 - 2 * (slab % 2)
    pair_a = core * (3 - slab) + (1 - core) * swap
    pair_b = core * swap + (1 - core) * (3 - slab)

    def offset(step):
        return (step * 13) % peers

    def peer(r):
        return ((x + r // 8) % 4) * 8 + ((z + (r // 2) % 4) % 4) * 2 + (core + r % 2) % 2

    def sh_copy(q):
        return pltpu.make_async_copy(
            shared.at[:, pl.ds(q * rows, rows), :], sh[q], sh_sem.at[q])

    def ow_copy(q):
        return pltpu.make_async_copy(
            owned.at[:, pl.ds(q * rows, rows), :], ow.at[q], ow_sem.at[q])

    def op_copy(i, s):
        return pltpu.make_async_copy(
            ops.at[pl.ds(s * lps, lps)], opv.at[i], op_sem.at[i])

    def out_copy(q):
        return pltpu.make_async_copy(
            outb.at[q], out.at[:, pl.ds(q * rows, rows), :], out_sem.at[q])

    def a_copy(q):
        return pltpu.make_async_remote_copy(
            dn.at[q], dp.at[q], as_sem.at[q], ar_sem.at[q],
            device_id=(pair_a, cube), device_id_type=MESH)

    def b_copy(q):
        return pltpu.make_async_remote_copy(
            pbs.at[q], pbr.at[q], bs_sem.at[q], br_sem.at[q],
            device_id=(pair_b, cube), device_id_type=MESH)

    def i_copy():
        return pltpu.make_async_remote_copy(
            inter_v, ipv, isend_sem, irecv_sem,
            device_id=(pair_b, cube), device_id_type=MESH)

    for q in range(chunks):
        sh_copy(q).start()
    for q in range(chunks):
        ow_copy(q).start()
    op_copy(0, slab).start()
    op_copy(1, pair_a).start()

    barrier = pltpu.get_barrier_semaphore()

    def greet(r, carry):
        pl.semaphore_signal(barrier, inc=1, device_id=(slab, peer(r)), device_id_type=MESH)
        return carry

    lax.fori_loop(1, peers, greet, 0)
    for s in (pair_a, pair_b):
        pl.semaphore_signal(barrier, inc=1, device_id=(s, cube), device_id_type=MESH)

    def pack(q, r, to):
        c = peer(r)
        for k in range(CAP):
            to[q, r, k] = sh[q][tab[c * CAP + k]]

    def pack_step(q, step, carry):
        pack(q, offset(step), send)
        return carry

    def send_step(q, step, carry):
        r = offset(step)
        pltpu.make_async_remote_copy(
            send.at[q, r], recv.at[q, r], send_sem.at[q], recv_sem.at[q],
            device_id=(slab, peer(r)), device_id_type=MESH).start()
        return carry

    def key_step(r, carry):
        c = peer(r)
        pltpu.make_async_remote_copy(
            keys.at[c], keyr.at[r], ksend_sem, krecv_sem,
            device_id=(slab, c), device_id_type=MESH).start()
        return carry

    for q in range(chunks):
        sh_copy(q).wait()
        pack(q, 0, recv)
        lax.fori_loop(1, peers, functools.partial(pack_step, q), 0)
        if q == 0:
            keyr[0] = keys[cube]
            pl.semaphore_wait(barrier, peers + 1)
            lax.fori_loop(1, peers, key_step, 0)
            i_copy().start()
        lax.fori_loop(1, peers, functools.partial(send_step, q), 0)

    far = pl.ds(1, peers - 1)

    def sum_chunk(q):
        pltpu.make_async_copy(recv.at[q, far], recv.at[q, far], recv_sem.at[q]).wait()
        ow_copy(q).wait()
        total = jnp.dot(
            kron[...], recv[q].reshape(peers * CAP * rows, width),
            preferred_element_type=jnp.float32)
        total = total + ow[q].reshape(octs * rows, width).astype(jnp.float32)
        dn[q] = total.astype(jnp.bfloat16).reshape(octs, rows, width)

    def products(i, src, q):
        def one(e, carry):
            prod = jnp.dot(
                src[q].reshape(octs * rows, width), opv[i, e],
                preferred_element_type=jnp.float32)
            y[i, pl.ds(e * octs, octs)] = prod.reshape(octs, rows, width)
            return carry
        lax.fori_loop(0, lps, one, 0)

    def gather(table, t):
        row, base = t // 4, (t % 4) * 32
        total = None
        for i, s in ((0, slab), (1, pair_a)):
            for e in range(lps):
                term = y[i, e * octs + table[row, base + s * lps + e]]
                total = term if total is None else total + term
        return total

    def finish(q):
        b_copy(q).wait_recv()
        outb[q] = (acc[q] + pbr[q].astype(jnp.float32)).astype(jnp.bfloat16)
        out_copy(q).start()

    for q in range(chunks):
        if q == 0:
            pltpu.make_async_copy(keyr.at[far], keyr.at[far], krecv_sem).wait()
            lane = lax.broadcasted_iota(jnp.int32, (1, 128), 1) // 32
            line = lax.broadcasted_iota(jnp.int32, (octs * rows, 128), 0)
            for g in range(peers // 4):
                key = keyr[4 * g]
                for b in range(1, 4):
                    key = jnp.where(lane == b, keyr[4 * g + b], key)
                kron[:, pl.ds(g * 128, 128)] = jnp.where(
                    key == line, 1.0, 0.0).astype(jnp.bfloat16)
        sum_chunk(q)
        a_copy(q).start()
        if q == 0:
            i_copy().wait_recv()
            to_smem = pltpu.make_async_copy(ipv, ips, ips_sem)
            to_smem.start()
            to_smem.wait()
            op_copy(0, slab).wait()
        else:
            finish(q - 1)
        products(0, dn, q)
        if q == 0:
            op_copy(1, pair_a).wait()
        a_copy(q).wait_recv()
        products(1, dp, q)

        def partner_target(t, carry, q=q):
            pbs[q, t] = gather(ips, t).astype(jnp.bfloat16)
            return carry

        lax.fori_loop(0, octs, partner_target, 0)
        b_copy(q).start()

        def own_target(t, carry, q=q):
            acc[q, t] = gather(inter_s, t)
            return carry

        lax.fori_loop(0, octs, own_target, 0)
    finish(chunks - 1)
    for q in range(chunks):
        pltpu.make_async_copy(send.at[q, far], send.at[q, far], send_sem.at[q]).wait()
        a_copy(q).wait_send()
        b_copy(q).wait_send()
        out_copy(q).wait()
    pltpu.make_async_copy(keyr.at[far], keyr.at[far], ksend_sem).wait()
    i_copy().wait_send()


def body(owned_part, shared_part, shared_cube, shared_octant, interaction, operators):
    octs, rhs, width = owned_part.shape
    slots = shared_part.shape[0]
    slabs, lps = interaction.shape[1:]
    cubes = lax.axis_size("cube")
    chunks = rhs // ROWS
    owner = shared_cube[:, 0]
    order = jnp.arange(slots, dtype=jnp.int32)
    earlier = (owner[:, None] == owner[None, :]) & (order[None, :] < order[:, None])
    rank = jnp.sum(earlier.astype(jnp.int32), axis=1)
    position = owner * CAP + rank
    placing = jnp.arange(cubes * CAP, dtype=jnp.int32)[:, None] == position[None, :]
    tab = jnp.sum(jnp.where(placing, order[None, :], 0), axis=1)
    label = jnp.sum(jnp.where(placing, shared_octant[None, :] + 1, 0), axis=1) - 1
    spread = jnp.arange(ROWS, dtype=jnp.int32)[None, None, None, :]
    label = label.reshape(cubes, 1, CAP, 1)
    keys = jnp.where(label >= 0, label * ROWS + spread, -1)
    keys = jnp.broadcast_to(keys, (cubes, 4, CAP, ROWS)).reshape(cubes, 1, 4 * CAP * ROWS)
    inter = interaction.reshape(octs // 4, 4 * slabs * lps)
    bf16, f32, dma = jnp.bfloat16, jnp.float32, pltpu.SemaphoreType.DMA
    block = (chunks, octs, ROWS, width)
    smem = pl.BlockSpec(memory_space=pltpu.SMEM)
    vmem = pl.BlockSpec(memory_space=pltpu.VMEM)
    hbm = pl.BlockSpec(memory_space=pl.ANY)
    return pl.pallas_call(
        kernel,
        out_shape=jax.ShapeDtypeStruct((octs, rhs, width), bf16),
        in_specs=[smem, smem, vmem, vmem, hbm, hbm, hbm],
        out_specs=hbm,
        scratch_shapes=[
            *[pltpu.VMEM((slots, ROWS, width), bf16) for _ in range(chunks)],
            pltpu.VMEM(block, bf16),
            pltpu.VMEM((2, lps, width, width), bf16),
            pltpu.VMEM((chunks, cubes, CAP, ROWS, width), bf16),
            pltpu.VMEM((chunks, cubes, CAP, ROWS, width), bf16),
            pltpu.VMEM((cubes, 1, 128), jnp.int32),
            pltpu.VMEM((octs * ROWS, cubes * CAP * ROWS), bf16),
            pltpu.VMEM(block, bf16),
            pltpu.VMEM(block, bf16),
            pltpu.VMEM((2, lps * octs, ROWS, width), f32),
            pltpu.VMEM(block, bf16),
            pltpu.VMEM(block, bf16),
            pltpu.VMEM(block, f32),
            pltpu.VMEM(block, bf16),
            pltpu.VMEM(inter.shape, jnp.int32),
            pltpu.SMEM(inter.shape, jnp.int32),
            dma((chunks,)), dma((chunks,)), dma((2,)), dma((chunks,)), dma((chunks,)),
            dma, dma, dma, dma, dma,
            dma((chunks,)), dma((chunks,)), dma((chunks,)), dma((chunks,)), dma((chunks,)),
        ],
        compiler_params=pltpu.CompilerParams(
            collective_id=0, has_side_effects=True, vmem_limit_bytes=56 * 2**20),
        cost_estimate=pl.CostEstimate(
            flops=2 * 2 * lps * octs * rhs * width * width,
            bytes_accessed=20 * 2**20, transcendentals=0),
    )(tab, inter, inter, keys, shared_part, owned_part, operators)


def solution(mesh):
    placed = (
        P(("slab", "cube"), None, None),
        P(("slab", "cube"), None, None),
        P(("slab", "cube"), None),
        P(("slab", "cube")),
        P(("slab", "cube"), None, None),
        P(),
    )
    return jax.shard_map(
        body, mesh=mesh, in_specs=placed, out_specs=P(("slab", "cube"), None, None), check_vma=False
    )
```

```python
import jax
import jax.numpy as jnp
from jax import lax
from jax.experimental import pallas as pl
from jax.experimental.pallas import tpu as pltpu
from jax.sharding import PartitionSpec as P

CAP = 2
ROWS = 16
AHEAD = 4
GROUP = 4
MESH = pl.DeviceIdType.MESH


def kernel(inter_s, inter_v, cube_row, octant_row, shared, owned, ops, out, *scratch):
    count = out.shape[1] // ROWS
    blocks = count
    rows = ROWS
    scratch = list(scratch)

    def take(n):
        taken = scratch[:n]
        del scratch[:n]
        return taken

    sh, ow, outb = take(blocks), take(blocks), take(blocks)
    send, recv = take(count), take(count)
    dn, dp, pbs, pbr, acc = take(count), take(count), take(count), take(count), take(count)
    opv, y, kron, tabv, tabs, keyv, keyr, ipv, ips = take(9)
    sh_sem, ow_sem, op_sem, out_sem, send_sem, recv_sem, as_sem, ar_sem, bs_sem, br_sem = take(10)
    ksend_sem, krecv_sem, isend_sem, irecv_sem, ips_sem, tab_sem = take(6)

    octs, _, width = out.shape
    slots = shared.shape[0]
    peers = keyr.shape[0]
    lps = opv.shape[1] * GROUP
    slab = lax.axis_index("slab")
    cube = lax.axis_index("cube")
    x, z, core = lax.div(cube, 8), lax.rem(lax.div(cube, 2), 4), lax.rem(cube, 2)
    swap = slab + 1 - 2 * lax.rem(slab, 2)
    pair_a = core * (3 - slab) + (1 - core) * swap
    pair_b = core * swap + (1 - core) * (3 - slab)

    at_x = [lax.rem(x + d, 4) * 8 for d in range(4)]
    at_z = [lax.rem(z + d, 4) * 2 for d in range(4)]
    at_core = [core, 1 - core]

    def peer(r):
        return at_x[r // 8] + at_z[r // 2 % 4] + at_core[r % 2]

    order = [step * 13 % peers for step in range(1, peers)]

    def sh_copy(b):
        return pltpu.make_async_copy(
            shared.at[:, pl.ds(b * ROWS, ROWS), :], sh[b], sh_sem.at[b])

    def ow_copy(b):
        return pltpu.make_async_copy(
            owned.at[:, pl.ds(b * ROWS, ROWS), :], ow[b], ow_sem.at[b])

    def op_copy(i, s, e):
        h, j = e // GROUP, e % GROUP
        return pltpu.make_async_copy(
            ops.at[s * lps + e], opv.at[i, h, :, pl.ds(j * width, width)], op_sem.at[i, e])

    def out_copy(b):
        return pltpu.make_async_copy(
            outb[b], out.at[:, pl.ds(b * ROWS, ROWS), :], out_sem.at[b])

    def a_copy(u):
        return pltpu.make_async_remote_copy(
            dn[u], dp[u], as_sem.at[u], ar_sem.at[u],
            device_id=(pair_a, cube), device_id_type=MESH)

    def b_copy(u):
        return pltpu.make_async_remote_copy(
            pbs[u], pbr[u], bs_sem.at[u], br_sem.at[u],
            device_id=(pair_b, cube), device_id_type=MESH)

    def i_copy():
        return pltpu.make_async_remote_copy(
            inter_v, ipv, isend_sem, irecv_sem,
            device_id=(pair_b, cube), device_id_type=MESH)

    for b in range(blocks):
        sh_copy(b).start()
    for b in range(blocks):
        ow_copy(b).start()
    for i, s in ((0, slab), (1, pair_a)):
        for e in range(lps):
            op_copy(i, s, e).start()

    barrier = pltpu.get_barrier_semaphore()

    for r in order:
        pl.semaphore_signal(barrier, inc=1, device_id=(slab, peer(r)), device_id_type=MESH)
    for s in (pair_a, pair_b):
        pl.semaphore_signal(barrier, inc=1, device_id=(s, cube), device_id_type=MESH)

    line = lax.broadcasted_iota(jnp.int32, (slots, slots), 0)
    lane = lax.broadcasted_iota(jnp.int32, (slots, slots), 1)

    def column(row):
        spread = jnp.broadcast_to(row, (slots, slots))
        return jnp.sum(jnp.where(line == lane, spread, 0), axis=1, keepdims=True)

    owner = cube_row[...]
    owner_col = column(owner)
    octant_col = column(octant_row[...])
    rank_col = jnp.sum(
        jnp.where((owner_col == owner) & (lane < line), 1, 0), axis=1, keepdims=True)
    for k in range(CAP):
        named = (owner_col == lane) & (rank_col == k)
        tabv[k:k + 1, 0:slots] = jnp.sum(jnp.where(named, line, 0), axis=0, keepdims=True)
    to_tabs = pltpu.make_async_copy(tabv, tabs, tab_sem)
    to_tabs.start()
    goes = jnp.where(owner == line, 1.0, 0.0).astype(jnp.bfloat16)
    wide = lax.broadcasted_iota(jnp.int32, (slots, 128), 1)
    value = jnp.where(rank_col == (wide // rows) % CAP, octant_col + 1, 0)
    label = jnp.dot(
        goes, value.astype(jnp.bfloat16),
        preferred_element_type=jnp.float32).astype(jnp.int32) - 1
    key = jnp.where(label >= 0, label * rows + wide % rows, -1)
    for c in range(peers):
        keyv[c] = key[c:c + 1, :]
    to_tabs.wait()

    def pack_unit(u):
        sh_copy(u).wait()
        for r in [0] + order:
            c = peer(r)
            to = send if r else recv
            for k in range(CAP):
                to[u][r, k * rows:(k + 1) * rows] = sh[u][tabs[k, c]]

    def send_unit(u):
        for r in order:
            pltpu.make_async_remote_copy(
                send[u].at[r], recv[u].at[r], send_sem.at[u], recv_sem.at[u],
                device_id=(slab, peer(r)), device_id_type=MESH).start()

    pack_unit(0)
    keyr[0] = keyv[cube]
    pl.semaphore_wait(barrier, peers + 1)
    for r in order:
        pltpu.make_async_remote_copy(
            keyv.at[peer(r)], keyr.at[r], ksend_sem, krecv_sem,
            device_id=(slab, peer(r)), device_id_type=MESH).start()
    i_copy().start()
    send_unit(0)
    for u in range(1, AHEAD):
        pack_unit(u)
        send_unit(u)

    far = pl.ds(1, peers - 1)

    def build():
        span = CAP * rows
        each = 128 // span
        spot = lax.broadcasted_iota(jnp.int32, (1, 128), 1) // span
        row = lax.broadcasted_iota(jnp.int32, (octs * rows, 128), 0)
        for g in range(peers // each):
            key = keyr[each * g]
            for i in range(1, each):
                key = jnp.where(spot == i, keyr[each * g + i], key)
            kron[:, pl.ds(g * 128, 128)] = jnp.where(key == row, 1.0, 0.0).astype(jnp.bfloat16)

    def sum_unit(u):
        pltpu.make_async_copy(recv[u].at[far], recv[u].at[far], recv_sem.at[u]).wait()
        ow_copy(u).wait()
        total = jnp.dot(
            kron[...], recv[u][...].reshape(peers * CAP * rows, width),
            preferred_element_type=jnp.float32)
        total = total + ow[u][...].reshape(octs * rows, width).astype(jnp.float32)
        dn[u][...] = total.astype(jnp.bfloat16)

    def products(i, u):
        src = (dn, dp)[i][u]

        def one(h, carry):
            prod = jnp.dot(src[...], opv[i, h], preferred_element_type=jnp.float32)
            for j in range(GROUP):
                y[i, pl.ds((h * GROUP + j) * octs, octs)] = prod[
                    :, j * width:(j + 1) * width].reshape(octs, rows, width)
            return carry

        lax.fori_loop(0, lps // GROUP, one, 0)

    def gather(table, t):
        total = None
        for i, s in ((0, slab), (1, pair_a)):
            for e in range(lps):
                term = y[i, e * octs + table[s * lps + e, t]]
                total = term if total is None else total + term
        return total

    def gather_partner(u):
        def step(t, carry):
            pbs[u][t] = gather(ips, t).astype(jnp.bfloat16)
            return carry

        lax.fori_loop(0, octs, step, 0)

    def gather_own(u):
        def step(t, carry):
            acc[u][t] = gather(inter_s, t)
            return carry

        lax.fori_loop(0, octs, step, 0)

    def finish(u):
        b_copy(u).wait_recv()
        outb[u][...] = (acc[u][...] + pbr[u][...].astype(jnp.float32)).astype(jnp.bfloat16)
        out_copy(u).start()

    def second(u):
        a_copy(u).wait_recv()
        products(1, u)
        gather_partner(u)
        b_copy(u).start()

    pltpu.make_async_copy(keyr.at[far], keyr.at[far], krecv_sem).wait()
    build()
    for u in range(count):
        sum_unit(u)
        a_copy(u).start()
        if u + AHEAD < count:
            pack_unit(u + AHEAD)
            send_unit(u + AHEAD)
        if u == 0:
            i_copy().wait_recv()
            to_smem = pltpu.make_async_copy(ipv, ips, ips_sem)
            to_smem.start()
            to_smem.wait()
            for i, s in ((0, slab), (1, pair_a)):
                for e in range(lps):
                    op_copy(i, s, e).wait()
        if 0 < u < count - 1:
            second(u - 1)
        if u > 0:
            gather_own(u - 1)
        if u > 1:
            finish(u - 2)
        products(0, u)
        if u >= count - 2:
            second(u)
    gather_own(count - 1)
    finish(count - 2)
    finish(count - 1)
    for u in range(count):
        pltpu.make_async_copy(send[u].at[far], send[u].at[far], send_sem.at[u]).wait()
        a_copy(u).wait_send()
        b_copy(u).wait_send()
    for b in range(blocks):
        out_copy(b).wait()
    pltpu.make_async_copy(keyv.at[far], keyv.at[far], ksend_sem).wait()
    i_copy().wait_send()


def body(owned_part, shared_part, shared_cube, shared_octant, interaction, operators):
    octs, rhs, width = owned_part.shape
    slots = shared_part.shape[0]
    slabs, lps = interaction.shape[1:]
    cubes = lax.axis_size("cube")
    blocks = count = rhs // ROWS
    inter = interaction.transpose(1, 2, 0).reshape(slabs * lps, octs)
    bf16, f32, i32, dma = jnp.bfloat16, jnp.float32, jnp.int32, pltpu.SemaphoreType.DMA
    smem = pl.BlockSpec(memory_space=pltpu.SMEM)
    vmem = pl.BlockSpec(memory_space=pltpu.VMEM)
    hbm = pl.BlockSpec(memory_space=pl.ANY)
    routed = [pltpu.VMEM((cubes, CAP * ROWS, width), bf16)] * count
    flat = [pltpu.VMEM((octs * ROWS, width), bf16)] * count
    partial = [pltpu.VMEM((octs, ROWS, width), bf16)] * count
    total = [pltpu.VMEM((octs, ROWS, width), f32)] * count
    return pl.pallas_call(
        kernel,
        out_shape=jax.ShapeDtypeStruct((octs, rhs, width), bf16),
        in_specs=[smem, vmem, vmem, vmem, hbm, hbm, hbm],
        out_specs=hbm,
        scratch_shapes=[
            *[pltpu.VMEM((slots, ROWS, width), bf16) for _ in range(blocks)],
            *[pltpu.VMEM((octs, ROWS, width), bf16) for _ in range(2 * blocks)],
            *routed, *routed, *flat, *flat, *partial, *partial, *total,
            pltpu.VMEM((2, lps // GROUP, width, GROUP * width), bf16),
            pltpu.VMEM((2, lps * octs, ROWS, width), f32),
            pltpu.VMEM((octs * ROWS, cubes * CAP * ROWS), bf16),
            pltpu.VMEM((8, 128), i32),
            pltpu.SMEM((8, 128), i32),
            pltpu.VMEM((cubes, 1, 128), i32),
            pltpu.VMEM((cubes, 1, 128), i32),
            pltpu.VMEM(inter.shape, i32),
            pltpu.SMEM(inter.shape, i32),
            dma((blocks,)), dma((blocks,)), dma((2, lps)), dma((blocks,)),
            *[dma((count,)) for _ in range(6)],
            *[dma for _ in range(6)],
        ],
        compiler_params=pltpu.CompilerParams(
            collective_id=0, has_side_effects=True, vmem_limit_bytes=56 * 2**20),
        cost_estimate=pl.CostEstimate(
            flops=2 * 2 * lps * octs * rhs * width * width,
            bytes_accessed=20 * 2**20, transcendentals=0),
    )(inter, inter, shared_cube.reshape(1, slots), shared_octant.reshape(1, slots),
      shared_part, owned_part, operators)


def solution(mesh):
    placed = (
        P(("slab", "cube"), None, None),
        P(("slab", "cube"), None, None),
        P(("slab", "cube"), None),
        P(("slab", "cube")),
        P(("slab", "cube"), None, None),
        P(),
    )
    return jax.shard_map(
        body, mesh=mesh, in_specs=placed, out_specs=P(("slab", "cube"), None, None), check_vma=False
    )
```

```python
import jax
import jax.numpy as jnp
from jax import lax
from jax.experimental import pallas as pl
from jax.experimental.pallas import tpu as pltpu
from jax.sharding import PartitionSpec as P

CAP = 2
ROWS = 16
UNITS = ((0, 0, 16), (1, 0, 16), (2, 0, 16), (3, 0, 8), (3, 8, 8))
GROUP = 4
MESH = pl.DeviceIdType.MESH


def kernel(inter, cube_row, octant_row, shared, owned, ops, out, *scratch):
    count = len(UNITS)
    blocks = out.shape[1] // ROWS
    scratch = list(scratch)

    def take(n):
        taken = scratch[:n]
        del scratch[:n]
        return taken

    sh, ow = take(blocks), take(blocks)
    send, recv = take(count), take(count)
    dn, dp, pbs, pbr, acc = take(count), take(count), take(count), take(count), take(count)
    opv, y, kron16, kron8, tabv, tabs, keyv, keyr, ipv, ips, inter_s = take(11)
    sh_sem, ow_sem, op_sem, send_sem, recv_sem, as_sem, ar_sem, bs_sem, br_sem = take(9)
    ksend_sem, krecv_sem, isend_sem, irecv_sem, ips_sem, tab_sem, ins_sem = take(7)

    octs, _, width = out.shape
    slots = shared.shape[0]
    peers = keyr.shape[0]
    lps = opv.shape[1] * GROUP
    slab = lax.axis_index("slab")
    cube = lax.axis_index("cube")
    x, z, core = lax.div(cube, 8), lax.rem(lax.div(cube, 2), 4), lax.rem(cube, 2)
    swap = slab + 1 - 2 * lax.rem(slab, 2)
    pair_a = core * (3 - slab) + (1 - core) * swap
    pair_b = core * swap + (1 - core) * (3 - slab)

    at_x = [lax.rem(x + d, 4) * 8 for d in range(4)]
    at_z = [lax.rem(z + d, 4) * 2 for d in range(4)]
    at_core = [core, 1 - core]

    def peer(r):
        return at_x[r // 8] + at_z[r // 2 % 4] + at_core[r % 2]

    order = [step * 13 % peers for step in range(1, peers)]

    def sh_copy(b):
        return pltpu.make_async_copy(
            shared.at[:, pl.ds(b * ROWS, ROWS), :], sh[b], sh_sem.at[b])

    def ow_copy(b):
        return pltpu.make_async_copy(
            owned.at[:, pl.ds(b * ROWS, ROWS), :], ow[b], ow_sem.at[b])

    def op_copy(i, s, e):
        h, j = e // GROUP, e % GROUP
        return pltpu.make_async_copy(
            ops.at[s * lps + e], opv.at[i, h, :, pl.ds(j * width, width)], op_sem.at[i, e])

    def a_copy(u):
        return pltpu.make_async_remote_copy(
            dn[u], dp[u], as_sem.at[u], ar_sem.at[u],
            device_id=(pair_a, cube), device_id_type=MESH)

    def b_copy(u):
        return pltpu.make_async_remote_copy(
            pbs[u], pbr[u], bs_sem.at[u], br_sem.at[u],
            device_id=(pair_b, cube), device_id_type=MESH)

    def i_copy():
        return pltpu.make_async_remote_copy(
            inter, ipv, isend_sem, irecv_sem,
            device_id=(pair_b, cube), device_id_type=MESH)

    sh_copy(0).start()
    barrier = pltpu.get_barrier_semaphore()

    for r in order:
        pl.semaphore_signal(barrier, inc=1, device_id=(slab, peer(r)), device_id_type=MESH)
    for s in (pair_a, pair_b):
        pl.semaphore_signal(barrier, inc=1, device_id=(s, cube), device_id_type=MESH)
    for b in range(1, blocks):
        sh_copy(b).start()

    line = lax.broadcasted_iota(jnp.int32, (slots, slots), 0)
    lane = lax.broadcasted_iota(jnp.int32, (slots, slots), 1)

    def column(row):
        spread = jnp.broadcast_to(row, (slots, slots))
        return jnp.sum(jnp.where(line == lane, spread, 0), axis=1, keepdims=True)

    owner = cube_row[...]
    owner_col = column(owner)
    octant_col = column(octant_row[...])
    rank_col = jnp.sum(
        jnp.where((owner_col == owner) & (lane < line), 1, 0), axis=1, keepdims=True)
    for k in range(CAP):
        named = (owner_col == lane) & (rank_col == k)
        tabv[k:k + 1, 0:slots] = jnp.sum(jnp.where(named, line, 0), axis=0, keepdims=True)
    to_tabs = pltpu.make_async_copy(tabv, tabs, tab_sem)
    to_tabs.start()
    to_tabs.wait()

    def pack_unit(u):
        b, first, rows = UNITS[u]
        if first == 0:
            sh_copy(b).wait()
        for r in [0] + order:
            c = peer(r)
            to = send if r else recv
            if rows == ROWS:
                for k in range(CAP):
                    to[u][r, k * rows:(k + 1) * rows] = sh[b][tabs[k, c]]
            else:
                parts = [
                    sh[b][tabs[k, c]].astype(jnp.float32)[first:first + rows]
                    for k in range(CAP)]
                to[u][r] = jnp.concatenate(parts, axis=0).astype(jnp.bfloat16)

    def send_unit(u):
        for r in order:
            pltpu.make_async_remote_copy(
                send[u].at[r], recv[u].at[r], send_sem.at[u], recv_sem.at[u],
                device_id=(slab, peer(r)), device_id_type=MESH).start()

    pack_unit(0)
    pl.semaphore_wait(barrier, peers + 1)
    send_unit(0)
    goes = jnp.where(owner == line, 1.0, 0.0).astype(jnp.bfloat16)
    wide = lax.broadcasted_iota(jnp.int32, (slots, 128), 1)
    for i, rows in enumerate((16, 8)):
        value = jnp.where(rank_col == (wide // rows) % CAP, octant_col + 1, 0)
        label = jnp.dot(
            goes, value.astype(jnp.bfloat16),
            preferred_element_type=jnp.float32).astype(jnp.int32) - 1
        key = jnp.where(label >= 0, label * rows + wide % rows, -1)
        for c in range(peers):
            keyv[c, i:i + 1, :] = key[c:c + 1, :]
    keyr[0] = keyv[cube]
    for r in order:
        pltpu.make_async_remote_copy(
            keyv.at[peer(r)], keyr.at[r], ksend_sem, krecv_sem,
            device_id=(slab, peer(r)), device_id_type=MESH).start()
    i_copy().start()
    to_inter = pltpu.make_async_copy(inter, inter_s, ins_sem)
    to_inter.start()
    for b in range(blocks):
        ow_copy(b).start()
    for i, s in ((0, slab), (1, pair_a)):
        for e in range(lps):
            op_copy(i, s, e).start()
    for u in range(1, count):
        pack_unit(u)
        send_unit(u)

    far = pl.ds(1, peers - 1)

    def build(kron, index, rows):
        span = CAP * rows
        each = 128 // span
        spot = lax.broadcasted_iota(jnp.int32, (1, 128), 1) // span
        row = lax.broadcasted_iota(jnp.int32, (octs * rows, 128), 0)
        for g in range(peers // each):
            key = keyr[each * g, index:index + 1, :]
            for i in range(1, each):
                key = jnp.where(spot == i, keyr[each * g + i, index:index + 1, :], key)
            kron[:, pl.ds(g * 128, 128)] = jnp.where(key == row, 1.0, 0.0).astype(jnp.bfloat16)

    def sum_unit(u):
        b, first, rows = UNITS[u]
        pltpu.make_async_copy(recv[u].at[far], recv[u].at[far], recv_sem.at[u]).wait()
        if first == 0:
            ow_copy(b).wait()
        kron = kron16 if rows == ROWS else kron8
        total = jnp.dot(
            kron[...], recv[u][...].reshape(peers * CAP * rows, width),
            preferred_element_type=jnp.float32)
        own = ow[b][...]
        if rows < ROWS:
            own = own.astype(jnp.float32)[:, first:first + rows]
        total = total + own.reshape(octs * rows, width).astype(jnp.float32)
        dn[u][...] = total.astype(jnp.bfloat16)

    def products(i, u):
        rows = UNITS[u][2]
        src = (dn, dp)[i][u]

        def one(h, carry):
            prod = jnp.dot(src[...], opv[i, h], preferred_element_type=jnp.float32)
            for j in range(GROUP):
                y[i, pl.ds((h * GROUP + j) * octs, octs), 0:rows] = prod[
                    :, j * width:(j + 1) * width].reshape(octs, rows, width)
            return carry

        lax.fori_loop(0, lps // GROUP, one, 0)

    def gather(table, t, rows):
        total = None
        for i, s in ((0, slab), (1, pair_a)):
            for e in range(lps):
                term = y[i, e * octs + table[s * lps + e, t], 0:rows]
                total = term if total is None else total + term
        return total

    def gather_partner(u):
        rows = UNITS[u][2]
        per = ROWS // rows

        def step(t, carry):
            parts = [gather(ips, per * t + i, rows) for i in range(per)]
            part = parts[0] if per == 1 else jnp.concatenate(parts, axis=0)
            pbs[u][t] = part.astype(jnp.bfloat16)
            return carry

        lax.fori_loop(0, octs // per, step, 0)

    def gather_own(u):
        rows = UNITS[u][2]
        per = ROWS // rows

        def step(t, carry):
            for i in range(per):
                acc[u][per * t + i] = gather(inter_s, per * t + i, rows)
            return carry

        lax.fori_loop(0, octs // per, step, 0)

    def finish(u):
        b, first, rows = UNITS[u]
        b_copy(u).wait_recv()
        total = acc[u][...] + pbr[u][...].astype(jnp.float32).reshape(octs, rows, width)
        if rows < ROWS and first == 0:
            acc[u][...] = total
            return
        if rows < ROWS:
            total = jnp.concatenate([acc[u - 1][...], total], axis=1)
        out[:, b * ROWS:(b + 1) * ROWS, :] = total.astype(jnp.bfloat16)

    def second(u):
        a_copy(u).wait_recv()
        products(1, u)
        gather_partner(u)
        b_copy(u).start()

    pltpu.make_async_copy(keyr.at[far], keyr.at[far], krecv_sem).wait()
    build(kron16, 0, 16)
    for u in range(count):
        sum_unit(u)
        a_copy(u).start()
        if u == 0:
            build(kron8, 1, 8)
            to_inter.wait()
            i_copy().wait_recv()
            to_smem = pltpu.make_async_copy(ipv, ips, ips_sem)
            to_smem.start()
            to_smem.wait()
            for i, s in ((0, slab), (1, pair_a)):
                for e in range(lps):
                    op_copy(i, s, e).wait()
        else:
            second(u - 1)
            gather_own(u - 1)
        products(0, u)
        if 1 < u < count - 1:
            finish(u - 2)
    second(count - 1)
    gather_own(count - 1)
    for u in range(count - 3, count):
        finish(u)
    for u in range(count):
        pltpu.make_async_copy(send[u].at[far], send[u].at[far], send_sem.at[u]).wait()
        a_copy(u).wait_send()
        b_copy(u).wait_send()
    pltpu.make_async_copy(keyv.at[far], keyv.at[far], ksend_sem).wait()
    i_copy().wait_send()


def body(owned_part, shared_part, shared_cube, shared_octant, interaction, operators):
    octs, rhs, width = owned_part.shape
    slots = shared_part.shape[0]
    slabs, lps = interaction.shape[1:]
    cubes = lax.axis_size("cube")
    blocks = rhs // ROWS
    count = len(UNITS)
    inter = interaction.transpose(1, 2, 0).reshape(slabs * lps, octs)
    bf16, f32, i32, dma = jnp.bfloat16, jnp.float32, jnp.int32, pltpu.SemaphoreType.DMA
    vmem = pl.BlockSpec(memory_space=pltpu.VMEM)
    hbm = pl.BlockSpec(memory_space=pl.ANY)
    routed = [pltpu.VMEM((cubes, CAP * rows, width), bf16) for _, _, rows in UNITS]
    flat = [pltpu.VMEM((octs * rows, width), bf16) for _, _, rows in UNITS]
    partial = [pltpu.VMEM((octs * rows // ROWS, ROWS, width), bf16) for _, _, rows in UNITS]
    total = [pltpu.VMEM((octs, rows, width), f32) for _, _, rows in UNITS]
    return pl.pallas_call(
        kernel,
        out_shape=pltpu.VMEM((octs, rhs, width), bf16),
        in_specs=[hbm, vmem, vmem, hbm, hbm, hbm],
        out_specs=vmem,
        scratch_shapes=[
            *[pltpu.VMEM((slots, ROWS, width), bf16) for _ in range(blocks)],
            *[pltpu.VMEM((octs, ROWS, width), bf16) for _ in range(blocks)],
            *routed, *routed, *flat, *flat, *partial, *partial, *total,
            pltpu.VMEM((2, lps // GROUP, width, GROUP * width), bf16),
            pltpu.VMEM((2, lps * octs, ROWS, width), f32),
            pltpu.VMEM((octs * 16, cubes * CAP * 16), bf16),
            pltpu.VMEM((octs * 8, cubes * CAP * 8), bf16),
            pltpu.VMEM((8, 128), i32),
            pltpu.SMEM((8, 128), i32),
            pltpu.VMEM((cubes, 2, 128), i32),
            pltpu.VMEM((cubes, 2, 128), i32),
            pltpu.VMEM(inter.shape, i32),
            pltpu.SMEM(inter.shape, i32),
            pltpu.SMEM(inter.shape, i32),
            dma((blocks,)), dma((blocks,)), dma((2, lps)),
            *[dma((count,)) for _ in range(6)],
            *[dma for _ in range(7)],
        ],
        compiler_params=pltpu.CompilerParams(
            collective_id=0, has_side_effects=True, vmem_limit_bytes=56 * 2**20),
        cost_estimate=pl.CostEstimate(
            flops=2 * 2 * lps * octs * rhs * width * width,
            bytes_accessed=20 * 2**20, transcendentals=0),
    )(inter, shared_cube.reshape(1, slots), shared_octant.reshape(1, slots),
      shared_part, owned_part, operators)


def solution(mesh):
    placed = (
        P(("slab", "cube"), None, None),
        P(("slab", "cube"), None, None),
        P(("slab", "cube"), None),
        P(("slab", "cube")),
        P(("slab", "cube"), None, None),
        P(),
    )
    return jax.shard_map(
        body, mesh=mesh, in_specs=placed, out_specs=P(("slab", "cube"), None, None), check_vma=False
    )
```

```python
import jax
import jax.numpy as jnp
from jax import lax
from jax.experimental import pallas as pl
from jax.experimental.pallas import tpu as pltpu
from jax.sharding import PartitionSpec as P

CAP = 2
ROWS = 16
UNITS = ((0, 0, 16), (1, 0, 16), (2, 0, 16), (3, 0, 8), (3, 8, 8))
GROUP = 4
MESH = pl.DeviceIdType.MESH


def kernel(inter, cube_row, octant_row, shared, owned, ops, out, *scratch):
    count = len(UNITS)
    blocks = out.shape[1] // ROWS
    scratch = list(scratch)

    def take(n):
        taken = scratch[:n]
        del scratch[:n]
        return taken

    sh, ow = take(blocks), take(blocks)
    send, recv = take(count), take(count)
    dn, dp, pbs, pbr, acc = take(count), take(count), take(count), take(count), take(count)
    opv, y, kron16, kron8, tabv, tabs, keyv, keyr, ipv, ips, inter_s = take(11)
    sh_sem, ow_sem, op_sem, send_sem, recv_sem, as_sem, ar_sem, bs_sem, br_sem = take(9)
    ksend_sem, krecv_sem, isend_sem, irecv_sem, ips_sem, tab_sem, ins_sem = take(7)

    octs, _, width = out.shape
    slots = shared.shape[0]
    peers = keyr.shape[0]
    lps = opv.shape[1] * GROUP
    slab = lax.axis_index("slab")
    cube = lax.axis_index("cube")
    x, z, core = lax.div(cube, 8), lax.rem(lax.div(cube, 2), 4), lax.rem(cube, 2)
    swap = slab + 1 - 2 * lax.rem(slab, 2)
    pair_a = core * (3 - slab) + (1 - core) * swap
    pair_b = core * swap + (1 - core) * (3 - slab)

    at_x = [lax.rem(x + d, 4) * 8 for d in range(4)]
    at_z = [lax.rem(z + d, 4) * 2 for d in range(4)]
    at_core = [core, 1 - core]

    def peer(r):
        return at_x[r // 8] + at_z[r // 2 % 4] + at_core[r % 2]

    order = [step * 13 % peers for step in range(1, peers)]

    def sh_copy(b):
        return pltpu.make_async_copy(
            shared.at[:, pl.ds(b * ROWS, ROWS), :], sh[b], sh_sem.at[b])

    def ow_copy(b):
        return pltpu.make_async_copy(
            owned.at[:, pl.ds(b * ROWS, ROWS), :], ow[b], ow_sem.at[b])

    def op_copy(i, s, e):
        h, j = e // GROUP, e % GROUP
        return pltpu.make_async_copy(
            ops.at[s * lps + e], opv.at[i, h, :, pl.ds(j * width, width)], op_sem.at[i, e])

    def a_copy(u):
        return pltpu.make_async_remote_copy(
            dn[u], dp[u], as_sem.at[u], ar_sem.at[u],
            device_id=(pair_a, cube), device_id_type=MESH)

    def b_copy(u):
        return pltpu.make_async_remote_copy(
            pbs[u], pbr[u], bs_sem.at[u], br_sem.at[u],
            device_id=(pair_b, cube), device_id_type=MESH)

    def i_copy():
        return pltpu.make_async_remote_copy(
            inter, ipv, isend_sem, irecv_sem,
            device_id=(pair_b, cube), device_id_type=MESH)

    sh_copy(0).start()
    barrier = pltpu.get_barrier_semaphore()

    for r in order:
        pl.semaphore_signal(barrier, inc=1, device_id=(slab, peer(r)), device_id_type=MESH)
    for s in (pair_a, pair_b):
        pl.semaphore_signal(barrier, inc=1, device_id=(s, cube), device_id_type=MESH)
    for b in range(1, blocks):
        sh_copy(b).start()

    line = lax.broadcasted_iota(jnp.int32, (slots, slots), 0)
    lane = lax.broadcasted_iota(jnp.int32, (slots, slots), 1)

    def column(row):
        spread = jnp.broadcast_to(row, (slots, slots))
        return jnp.sum(jnp.where(line == lane, spread, 0), axis=1, keepdims=True)

    owner = cube_row[...]
    owner_col = column(owner)
    octant_col = column(octant_row[...])
    rank_col = jnp.sum(
        jnp.where((owner_col == owner) & (lane < line), 1, 0), axis=1, keepdims=True)
    for k in range(CAP):
        named = (owner_col == lane) & (rank_col == k)
        tabv[k:k + 1, 0:slots] = jnp.sum(jnp.where(named, line, 0), axis=0, keepdims=True)
    to_tabs = pltpu.make_async_copy(tabv, tabs, tab_sem)
    to_tabs.start()
    to_tabs.wait()

    def pack_unit(u):
        b, first, rows = UNITS[u]
        if first == 0:
            sh_copy(b).wait()
        for r in [0] + order:
            c = peer(r)
            to = send if r else recv
            if rows == ROWS:
                for k in range(CAP):
                    to[u][r, k * rows:(k + 1) * rows] = sh[b][tabs[k, c]]
            else:
                parts = [
                    sh[b][tabs[k, c]].astype(jnp.float32)[first:first + rows]
                    for k in range(CAP)]
                to[u][r] = jnp.concatenate(parts, axis=0).astype(jnp.bfloat16)

    def send_unit(u):
        for r in order:
            pltpu.make_async_remote_copy(
                send[u].at[r], recv[u].at[r], send_sem.at[u], recv_sem.at[u],
                device_id=(slab, peer(r)), device_id_type=MESH).start()

    pack_unit(0)
    pl.semaphore_wait(barrier, peers + 1)
    send_unit(0)
    goes = jnp.where(owner == line, 1.0, 0.0).astype(jnp.bfloat16)
    wide = lax.broadcasted_iota(jnp.int32, (slots, 128), 1)
    for i, rows in enumerate((16, 8)):
        value = jnp.where(rank_col == (wide // rows) % CAP, octant_col + 1, 0)
        label = jnp.dot(
            goes, value.astype(jnp.bfloat16),
            preferred_element_type=jnp.float32).astype(jnp.int32) - 1
        key = jnp.where(label >= 0, label * rows + wide % rows, -1)
        for c in range(peers):
            keyv[c, i:i + 1, :] = key[c:c + 1, :]
    keyr[0] = keyv[cube]
    for r in order:
        pltpu.make_async_remote_copy(
            keyv.at[peer(r)], keyr.at[r], ksend_sem, krecv_sem,
            device_id=(slab, peer(r)), device_id_type=MESH).start()
    i_copy().start()
    to_inter = pltpu.make_async_copy(inter, inter_s, ins_sem)
    to_inter.start()
    for b in range(blocks):
        ow_copy(b).start()
    for i, s in ((0, slab), (1, pair_a)):
        for e in range(lps):
            op_copy(i, s, e).start()
    for u in range(1, count):
        pack_unit(u)
        send_unit(u)

    far = pl.ds(1, peers - 1)

    def build(kron, index, rows):
        span = CAP * rows
        each = 128 // span
        spot = lax.broadcasted_iota(jnp.int32, (1, 128), 1) // span
        row = lax.broadcasted_iota(jnp.int32, (octs * rows, 128), 0)
        for g in range(peers // each):
            key = keyr[each * g, index:index + 1, :]
            for i in range(1, each):
                key = jnp.where(spot == i, keyr[each * g + i, index:index + 1, :], key)
            kron[:, pl.ds(g * 128, 128)] = jnp.where(key == row, 1.0, 0.0).astype(jnp.bfloat16)

    def sum_unit(u):
        b, first, rows = UNITS[u]
        pltpu.make_async_copy(recv[u].at[far], recv[u].at[far], recv_sem.at[u]).wait()
        if first == 0:
            ow_copy(b).wait()
        kron = kron16 if rows == ROWS else kron8
        total = jnp.dot(
            kron[...], recv[u][...].reshape(peers * CAP * rows, width),
            preferred_element_type=jnp.float32)
        own = ow[b][...]
        if rows < ROWS:
            own = own.astype(jnp.float32)[:, first:first + rows]
        total = total + own.reshape(octs * rows, width).astype(jnp.float32)
        dn[u][...] = total.astype(jnp.bfloat16)

    def products(i, u):
        rows = UNITS[u][2]
        src = (dn, dp)[i][u]

        def one(h, carry):
            prod = jnp.dot(src[...], opv[i, h], preferred_element_type=jnp.float32)
            for j in range(GROUP):
                y[i, pl.ds((h * GROUP + j) * octs, octs), 0:rows] = prod[
                    :, j * width:(j + 1) * width].reshape(octs, rows, width)
            return carry

        lax.fori_loop(0, lps // GROUP, one, 0)

    def gather(table, t, rows):
        total = None
        for i, s in ((0, slab), (1, pair_a)):
            for e in range(lps):
                term = y[i, e * octs + table[s * lps + e, t], 0:rows]
                total = term if total is None else total + term
        return total

    def gather_partner(u):
        rows = UNITS[u][2]
        per = ROWS // rows

        def step(i, carry):
            for t in (2 * i, 2 * i + 1):
                parts = [gather(ips, per * t + n, rows) for n in range(per)]
                part = parts[0] if per == 1 else jnp.concatenate(parts, axis=0)
                pbs[u][t] = part.astype(jnp.bfloat16)
            return carry

        lax.fori_loop(0, octs // per // 2, step, 0)

    def gather_own(u):
        rows = UNITS[u][2]
        per = 2 * ROWS // rows

        def step(t, carry):
            for i in range(per):
                acc[u][per * t + i] = gather(inter_s, per * t + i, rows)
            return carry

        lax.fori_loop(0, octs // per, step, 0)

    def finish(u):
        b, first, rows = UNITS[u]
        b_copy(u).wait_recv()
        total = acc[u][...] + pbr[u][...].astype(jnp.float32).reshape(octs, rows, width)
        if rows < ROWS and first == 0:
            acc[u][...] = total
            return
        if rows < ROWS:
            total = jnp.concatenate([acc[u - 1][...], total], axis=1)
        out[:, b * ROWS:(b + 1) * ROWS, :] = total.astype(jnp.bfloat16)

    def second(u):
        a_copy(u).wait_recv()
        products(1, u)
        gather_partner(u)
        b_copy(u).start()

    pltpu.make_async_copy(keyr.at[far], keyr.at[far], krecv_sem).wait()
    build(kron16, 0, 16)
    for u in range(count):
        sum_unit(u)
        a_copy(u).start()
        if u == 0:
            build(kron8, 1, 8)
            to_inter.wait()
            i_copy().wait_recv()
            to_smem = pltpu.make_async_copy(ipv, ips, ips_sem)
            to_smem.start()
            to_smem.wait()
            for i, s in ((0, slab), (1, pair_a)):
                for e in range(lps):
                    op_copy(i, s, e).wait()
        else:
            second(u - 1)
            gather_own(u - 1)
        products(0, u)
        if 1 < u < count - 1:
            finish(u - 2)
    second(count - 1)
    gather_own(count - 1)
    for u in range(count - 3, count):
        finish(u)
    for u in range(count):
        pltpu.make_async_copy(send[u].at[far], send[u].at[far], send_sem.at[u]).wait()
        a_copy(u).wait_send()
        b_copy(u).wait_send()
    pltpu.make_async_copy(keyv.at[far], keyv.at[far], ksend_sem).wait()
    i_copy().wait_send()


def body(owned_part, shared_part, shared_cube, shared_octant, interaction, operators):
    octs, rhs, width = owned_part.shape
    slots = shared_part.shape[0]
    slabs, lps = interaction.shape[1:]
    cubes = lax.axis_size("cube")
    blocks = rhs // ROWS
    count = len(UNITS)
    inter = interaction.transpose(1, 2, 0).reshape(slabs * lps, octs)
    bf16, f32, i32, dma = jnp.bfloat16, jnp.float32, jnp.int32, pltpu.SemaphoreType.DMA
    vmem = pl.BlockSpec(memory_space=pltpu.VMEM)
    hbm = pl.BlockSpec(memory_space=pl.ANY)
    routed = [pltpu.VMEM((cubes, CAP * rows, width), bf16) for _, _, rows in UNITS]
    flat = [pltpu.VMEM((octs * rows, width), bf16) for _, _, rows in UNITS]
    partial = [pltpu.VMEM((octs * rows // ROWS, ROWS, width), bf16) for _, _, rows in UNITS]
    total = [pltpu.VMEM((octs, rows, width), f32) for _, _, rows in UNITS]
    return pl.pallas_call(
        kernel,
        out_shape=pltpu.VMEM((octs, rhs, width), bf16),
        in_specs=[hbm, vmem, vmem, hbm, hbm, hbm],
        out_specs=vmem,
        scratch_shapes=[
            *[pltpu.VMEM((slots, ROWS, width), bf16) for _ in range(blocks)],
            *[pltpu.VMEM((octs, ROWS, width), bf16) for _ in range(blocks)],
            *routed, *routed, *flat, *flat, *partial, *partial, *total,
            pltpu.VMEM((2, lps // GROUP, width, GROUP * width), bf16),
            pltpu.VMEM((2, lps * octs, ROWS, width), f32),
            pltpu.VMEM((octs * 16, cubes * CAP * 16), bf16),
            pltpu.VMEM((octs * 8, cubes * CAP * 8), bf16),
            pltpu.VMEM((8, 128), i32),
            pltpu.SMEM((8, 128), i32),
            pltpu.VMEM((cubes, 2, 128), i32),
            pltpu.VMEM((cubes, 2, 128), i32),
            pltpu.VMEM(inter.shape, i32),
            pltpu.SMEM(inter.shape, i32),
            pltpu.SMEM(inter.shape, i32),
            dma((blocks,)), dma((blocks,)), dma((2, lps)),
            *[dma((count,)) for _ in range(6)],
            *[dma for _ in range(7)],
        ],
        compiler_params=pltpu.CompilerParams(
            collective_id=0, has_side_effects=True, vmem_limit_bytes=56 * 2**20),
        cost_estimate=pl.CostEstimate(
            flops=2 * 2 * lps * octs * rhs * width * width,
            bytes_accessed=20 * 2**20, transcendentals=0),
    )(inter, shared_cube.reshape(1, slots), shared_octant.reshape(1, slots),
      shared_part, owned_part, operators)


def solution(mesh):
    placed = (
        P(("slab", "cube"), None, None),
        P(("slab", "cube"), None, None),
        P(("slab", "cube"), None),
        P(("slab", "cube")),
        P(("slab", "cube"), None, None),
        P(),
    )
    return jax.shard_map(
        body, mesh=mesh, in_specs=placed, out_specs=P(("slab", "cube"), None, None), check_vma=False
    )
```
